32 devices in a mesh: fsdp: 32 (over z, y, x, core).
Axes of the slice: x: 2, y: 2, z: 4, core: 2. Of those that a mesh axis runs over, the one named last changes fastest.
Arguments:
- tokens: bfloat16 [4096, 768], P('fsdp'), may hold values from -6 to 6
- cotangent: bfloat16 [4096, 768], P('fsdp'), may hold values from -6 to 6
- lengths: int32 [64], replicated, may hold values from 1 to 127, as said below
- owner: int32 [64], replicated, may hold values from 0 to 31, as said below
- offsets: int32 [64], replicated, may hold values from 0 to 127, as said below
- ln1_gain: bfloat16 [768], P('fsdp'), may hold values from 0.099609375 to 1.8984375
- ln1_bias: bfloat16 [768], P('fsdp'), may hold values from -1.796875 to 1.796875
- w_qkv: bfloat16 [768, 2304], P('fsdp'), may hold values from -0.21875 to 0.21875
- b_query: bfloat16 [768], P('fsdp'), may hold values from -1.796875 to 1.796875
- b_value: bfloat16 [768], P('fsdp'), may hold values from -1.796875 to 1.796875
- w_proj: bfloat16 [768, 768], P('fsdp'), may hold values from -0.625 to 0.625
- b_proj: bfloat16 [768], P('fsdp'), may hold values from -1.796875 to 1.796875
- ln2_gain: bfloat16 [768], P('fsdp'), may hold values from 0.099609375 to 1.8984375
- ln2_bias: bfloat16 [768], P('fsdp'), may hold values from -1.796875 to 1.796875
- w_fc: bfloat16 [768, 3072], P('fsdp'), may hold values from -0.21875 to 0.21875
- b_fc: bfloat16 [3072], P('fsdp'), may hold values from -1.796875 to 1.796875
- w_out: bfloat16 [3072, 768], P('fsdp'), may hold values from -0.21875 to 0.21875
- b_out: bfloat16 [768], P('fsdp'), may hold values from -1.796875 to 1.796875
Outputs:
- result: bfloat16 [4096, 768], P('fsdp')
- grad_tokens: bfloat16 [4096, 768], P('fsdp')
- grad_ln1_gain: float32 [768], P('fsdp')
- grad_ln1_bias: float32 [768], P('fsdp')
- grad_w_qkv: float32 [768, 2304], P('fsdp')
- grad_b_query: float32 [768], P('fsdp')
- grad_b_value: float32 [768], P('fsdp')
- grad_w_proj: float32 [768, 768], P('fsdp')
- grad_b_proj: float32 [768], P('fsdp')
- grad_ln2_gain: float32 [768], P('fsdp')
- grad_ln2_bias: float32 [768], P('fsdp')
- grad_w_fc: float32 [768, 3072], P('fsdp')
- grad_b_fc: float32 [3072], P('fsdp')
- grad_w_out: float32 [3072, 768], P('fsdp')
- grad_b_out: float32 [768], P('fsdp')
The draws below stay inside these ranges and needn't reach their ends.
Inputs may be any that keep to these rules, and one draw needn't show every extreme that they name: Each device owns exactly two sequences, placed one after the other from slot 0 of its slots; their lengths add up to at most 128, and on some device to exactly 128. `owner`: every device owns exactly two sequences. `offsets`: A device's first sequence starts at slot 0, its second right after the first.
All inputs are finite; a program needn't handle non-finite values.
Results may differ from the reference program's by a relative error of at most 0.012.
Values may be sent and summed in bfloat16 or wider, within the bound.
A program may use at most 192 MiB of HBM per device.

```python
import jax
import jax.numpy as jnp
from jax import lax

D = 768
H = 12
HD = 64
FF = 3072
CAP = 128
SEQS = 64
TOKENS = 4096
N_FSDP = 32


def layout_draw(key):
    first_key, second_key, third_key, fourth_key = jax.random.split(key, 4)
    device_count = SEQS // 2
    positions = jnp.arange(device_count, dtype=jnp.int32)
    device_loads = jax.random.randint(first_key, (device_count,), CAP // 4, CAP + 1)
    fullest = jax.random.randint(second_key, (), 0, device_count)
    device_loads = jnp.where(positions == fullest, CAP, device_loads)
    leading = jax.random.randint(third_key, (device_count,), 1, device_loads)
    leading = jnp.where(positions == fullest, CAP - 1, leading)
    trailing = device_loads - leading
    sequence_lengths = jnp.stack([leading, trailing], axis=1).reshape(-1)
    start_slots = jnp.stack([jnp.zeros_like(leading), leading], axis=1).reshape(-1)
    owner_ids = jnp.repeat(positions, 2)
    shuffle = jax.random.permutation(fourth_key, SEQS)
    return (sequence_lengths[shuffle].astype(jnp.int32), owner_ids[shuffle].astype(jnp.int32), start_slots[shuffle].astype(jnp.int32))


def draw_lengths(key, part):
    return layout_draw(key)[0]


def draw_owner(key, part):
    return layout_draw(key)[1]


def draw_offsets(key, part):
    return layout_draw(key)[2]


def level_of(stream_key, shape, cuts, least, top_value):
    def one(dim, shards_of):
        draws = jax.random.uniform(jax.random.fold_in(jax.random.fold_in(stream_key, 6), dim), (shards_of,), jnp.float32, least / len(cuts), top_value / len(cuts))
        return jnp.repeat(jnp.exp(draws), shape[dim] // shards_of).reshape((-1,) + (1,) * (len(shape) - dim - 1))

    level = one(*cuts[0])
    for cut in cuts[1:]:
        level = level * one(*cut)
    return level


def bell_draw(stream_key, extent, scale, reach, shards=(), kind=jnp.bfloat16):
    array = scale * jax.random.normal(stream_key, extent, jnp.float32)
    if shards:
        array = array * level_of(stream_key, extent, shards, -0.22, 0.18)
    return jnp.clip(array, -reach, reach).astype(kind)


def setup_inputs(seed: int = 0) -> dict:
    seeds = jax.random.split(jax.random.key(seed), 19)
    tokens = bell_draw(seeds[0], (TOKENS, D), 1.0, 6.0, ((0, 32),))
    cotangent = bell_draw(seeds[1], (TOKENS, D), 1.0, 6.0, ((0, 32),))
    lengths = draw_lengths(jax.random.fold_in(seeds[18], 71), 0)
    owner = draw_owner(jax.random.fold_in(seeds[18], 71), 0)
    offsets = draw_offsets(jax.random.fold_in(seeds[18], 71), 0)
    ln1_gain = jnp.clip(1.0 + 0.18 * jax.random.normal(seeds[5], (D,), jnp.float32), 0.099609375, 1.8984375).astype(jnp.bfloat16)
    ln1_bias = bell_draw(seeds[6], (D,), 0.3, 1.796875, ((0, 32),))
    w_qkv = bell_draw(seeds[7], (D, 3 * D), D ** -0.5, 0.21875, ((0, 32),))
    b_query = bell_draw(seeds[8], (D,), 0.3, 1.796875, ((0, 32),))
    b_value = bell_draw(seeds[9], (D,), 0.3, 1.796875, ((0, 32),))
    w_proj = bell_draw(seeds[10], (D, D), (D // 8) ** -0.5, 0.625, ((0, 32),))
    b_proj = bell_draw(seeds[11], (D,), 0.3, 1.796875, ((0, 32),))
    ln2_gain = jnp.clip(1.0 + 0.18 * jax.random.normal(seeds[12], (D,), jnp.float32), 0.099609375, 1.8984375).astype(jnp.bfloat16)
    ln2_bias = bell_draw(seeds[13], (D,), 0.3, 1.796875, ((0, 32),))
    w_fc = bell_draw(seeds[14], (D, FF), D ** -0.5, 0.21875, ((0, 32),))
    b_fc = bell_draw(seeds[15], (FF,), 0.3, 1.796875, ((0, 32),))
    w_out = bell_draw(seeds[16], (FF, D), (FF // 4) ** -0.5, 0.21875, ((0, 32),))
    b_out = bell_draw(seeds[17], (D,), 0.3, 1.796875, ((0, 32),))
    return dict(tokens=tokens, cotangent=cotangent, lengths=lengths, owner=owner, offsets=offsets, ln1_gain=ln1_gain, ln1_bias=ln1_bias, w_qkv=w_qkv, b_query=b_query, b_value=b_value, w_proj=w_proj, b_proj=b_proj, ln2_gain=ln2_gain, ln2_bias=ln2_bias, w_fc=w_fc, b_fc=b_fc, w_out=w_out, b_out=b_out)


@jax.custom_vjp
def low(v):
    return lax.optimization_barrier(v.astype(jnp.bfloat16)).astype(jnp.float32)

@jax.custom_vjp
def low_back(v):
    return v

def low_keep(v):
    return (low(v), None)

def low_pass(kept, grad):
    return (grad,)

def back_keep(v):
    return (v, None)

def back_low(kept, grad):
    return (low(grad),)
low.defvjp(low_keep, low_pass)
low_back.defvjp(back_keep, back_low)
highest = lax.Precision.HIGHEST

def layer_norm(values, gain, shift):
    center = values - lax.optimization_barrier(jnp.mean(values, axis=-1, keepdims=True))
    spread = lax.optimization_barrier(jnp.mean(center * center, axis=-1, keepdims=True))
    return center * lax.rsqrt(spread + 1e-05) * gain + shift

def gelu_tanh(values):
    return 0.5 * values * (1.0 + jnp.tanh(0.7978845608028654 * (values + 0.044715 * values * values * values)))

def segment_ids(lengths, owner, offsets, device):
    slots = jnp.arange(CAP, dtype=jnp.int32)
    inside = (owner[:, None] == device) & (offsets[:, None] <= slots[None, :]) & (slots[None, :] < (offsets + lengths)[:, None])
    numbers = jnp.arange(SEQS, dtype=jnp.int32)[:, None] + 1
    return lax.optimization_barrier(jnp.sum(jnp.where(inside, numbers, 0), axis=0)).astype(jnp.int32) - 1

def block(inputs, labels, params):
    gain_one, shift_one, w_joined, bias_query, bias_value, w_project, bias_project, gain_two, shift_two, w_hidden, bias_hidden, w_final, bias_final = params
    normed = low(layer_norm(inputs, gain_one, shift_one))
    joined = jnp.dot(normed, w_joined, precision=highest)
    query = low_back(low(joined[:, :D] + bias_query)).reshape(CAP, H, HD)
    keys = low_back(low(joined[:, D:2 * D])).reshape(CAP, H, HD)
    values = low_back(low(joined[:, 2 * D:] + bias_value)).reshape(CAP, H, HD)
    scores = low_back(jnp.einsum('qhd,khd->hqk', query, keys, precision=highest) * 0.125)
    slots = jnp.arange(CAP, dtype=jnp.int32)
    allowed = (labels[:, None] == labels[None, :]) & (slots[None, :] <= slots[:, None])
    scores = jnp.where(allowed[None], scores, -1e+30)
    probs = low(jax.nn.softmax(scores, axis=-1))
    mixed = jnp.einsum('hqk,khd->qhd', probs, values, precision=highest).reshape(CAP, D)
    mixed = low_back(low(mixed))
    branch = low_back(jnp.dot(mixed, w_project, precision=highest) + bias_project)
    middle = inputs + branch
    second = low(layer_norm(middle, gain_two, shift_two))
    hidden = low_back(jnp.dot(second, w_hidden, precision=highest) + bias_hidden)
    active = low(gelu_tanh(hidden))
    return middle + low_back(jnp.dot(active, w_final, precision=highest) + bias_final)

def reference(tokens, cotangent, lengths, owner, offsets, ln1_gain, ln1_bias, w_qkv, b_query, b_value, w_proj, b_proj, ln2_gain, ln2_bias, w_fc, b_fc, w_out, b_out):
    params = tuple((tensor.astype(jnp.float32) for tensor in (ln1_gain, ln1_bias, w_qkv, b_query, b_value, w_proj, b_proj, ln2_gain, ln2_bias, w_fc, b_fc, w_out, b_out)))
    labels = lax.map(lambda device: segment_ids(lengths, owner, offsets, device), jnp.arange(N_FSDP, dtype=jnp.int32))
    inputs = tokens.astype(jnp.float32).reshape(N_FSDP, CAP, D)
    checked = jax.checkpoint(block)

    def forward(stacked, weights):
        return lax.map(lambda paired: checked(paired[0], paired[1], weights), (stacked, labels))
    outputs, pullback = jax.vjp(forward, inputs, params)
    valid = (labels >= 0).astype(jnp.float32)[..., None]
    seed_grad = cotangent.astype(jnp.float32).reshape(N_FSDP, CAP, D) * valid
    grad_inputs, grads = pullback(seed_grad)
    return (outputs.reshape(TOKENS, D).astype(jnp.bfloat16), grad_inputs.reshape(TOKENS, D).astype(jnp.bfloat16), grads[0], grads[1], grads[2], grads[3], grads[4], grads[5], grads[6], grads[7], grads[8], grads[9], grads[10], grads[11], grads[12])
```

```python
import jax
import jax.numpy as jnp
from jax import lax
from jax.experimental import pallas as pl
from jax.experimental.pallas import tpu as pltpu
from jax.sharding import PartitionSpec as P

H = 12
HD = 64


gelu_scale = 0.7978845608028654


def norm_forward(values, gain, shift):
    center = values - jnp.mean(values, axis=-1, keepdims=True)
    inv_std = lax.rsqrt(jnp.mean(center * center, axis=-1, keepdims=True) + 1e-05)
    normal = center * inv_std
    return (normal * gain + shift, normal, inv_std)


def norm_backward(upstream, normal, inv_std, gain):
    grad_gain = jnp.sum(upstream * normal, axis=0)
    grad_shift = jnp.sum(upstream, axis=0)
    scaled = upstream * gain
    inner = (
        scaled
        - jnp.mean(scaled, axis=-1, keepdims=True)
        - normal * jnp.mean(scaled * normal, axis=-1, keepdims=True)
    )
    return (inner * inv_std, grad_gain, grad_shift)


def outer_sum(left, right):
    return lax.dot_general(
        left, right, (((0,), (0,)), ((), ())), preferred_element_type=jnp.float32
    )


def through(left, weight):
    return lax.dot_general(
        left, weight, (((1,), (1,)), ((), ())), preferred_element_type=jnp.float32
    )


def column_sum(values):
    return jnp.sum(values.astype(jnp.float32), axis=0)


MESH = pl.DeviceIdType.MESH
SMALL_ROWS = 16
LANES = 128

PIECES = (
    (0, 0, None, 0),
    (1, 0, None, 0),
    (3, 0, 2, 0),
    (4, 0, None, 0),
    (2, 0, None, 1),
    (3, 1, 2, 1),
)


def place(device):
    return (device // 8, (device // 4) % 2, (device // 2) % 2, device % 2)


def moved(device, zm, fy, fx, fc):
    z, y, x, c = place(device)
    z_new = ((z // 2 + zm // 2) % 2) * 2 + (z + zm) % 2
    return z_new * 8 + ((y + fy) % 2) * 4 + ((x + fx) % 2) * 2 + (c + fc) % 2


def mask_of(order, zm, second, third, core):
    fy, fx = (second, third) if order == 0 else (third, second)
    return (zm, fy, fx, core)


def code(mask):
    zm, fy, fx, fc = mask
    return zm * 8 + fy * 4 + fx * 2 + fc


def view(ref, lead, piece):
    _, part, parts, _ = piece
    if parts is None:
        return ref.at[lead] if lead is not None else ref
    rows = ref.shape[-2] // parts
    if lead is None:
        return ref.at[pl.ds(part * rows, rows)]
    return ref.at[lead, pl.ds(part * rows, rows)]


def greet(device):
    barrier = pltpu.get_barrier_semaphore()
    peers = [(1, 0, 0, 0), (2, 0, 0, 0), (3, 0, 0, 0), (0, 1, 0, 0), (0, 0, 1, 0), (0, 0, 0, 1)]
    for peer in peers:
        pl.semaphore_signal(
            barrier, inc=1, device_id=(moved(device, *peer),), device_id_type=MESH
        )
    pl.semaphore_wait(barrier, len(peers))


def gather_kernel(*refs):
    shards, wholes = refs[:5], refs[5:10]
    send_sem, recv_sem, own_sem = refs[10:]
    device = lax.axis_index("fsdp")
    greet(device)

    def send(number, held, step):
        piece = PIECES[number]
        whole = wholes[piece[0]]
        origin = moved(device, *held)
        slot = code(held) + code(step)
        mine = isinstance(held[0], int) and held == (0, 0, 0, 0)
        source = view(shards[piece[0]], None, piece) if mine else view(whole, origin, piece)
        return pltpu.make_async_remote_copy(
            src_ref=source,
            dst_ref=view(whole, origin, piece),
            send_sem=send_sem.at[number, slot],
            recv_sem=recv_sem.at[number, slot],
            device_id=(moved(device, *step),),
            device_id_type=MESH,
        )

    def arrived(number, mask):
        piece = PIECES[number]
        target = view(wholes[piece[0]], moved(device, *mask), piece)
        return pltpu.make_async_remote_copy(
            src_ref=target,
            dst_ref=target,
            send_sem=send_sem.at[number, code(mask)],
            recv_sem=recv_sem.at[number, code(mask)],
            device_id=(moved(device, 0, 0, 0, 1),),
            device_id_type=MESH,
        )

    own = [
        pltpu.make_async_copy(shards[k], wholes[k].at[device], own_sem.at[k]) for k in range(5)
    ]
    home = (0, 0, 0, 0)
    pieces = range(len(PIECES))
    for step in (3, 1, 2):
        for n in pieces:
            send(n, home, (step, 0, 0, 0)).start()
    for n in pieces:
        order = PIECES[n][3]
        send(n, home, mask_of(order, 0, 1, 0, 0)).start()
        send(n, home, mask_of(order, 0, 0, 1, 0)).start()
        send(n, home, (0, 0, 0, 1)).start()
    for copy in own:
        copy.start()

    def second(zm):
        for n in pieces:
            order = PIECES[n][3]
            held = mask_of(order, zm, 1, 0, 0)
            arrived(n, held).wait_recv()
            send(n, held, mask_of(order, 0, 0, 1, 0)).start()
            send(n, held, (0, 0, 0, 1)).start()

    def along(zm):
        for n in pieces:
            order = PIECES[n][3]
            held = (zm, 0, 0, 0)
            arrived(n, held).wait_recv()
            send(n, held, mask_of(order, 0, 1, 0, 0)).start()
            send(n, held, mask_of(order, 0, 0, 1, 0)).start()
            send(n, held, (0, 0, 0, 1)).start()

    def third(k):
        for n in pieces:
            held = mask_of(PIECES[n][3], k % 4, k // 4, 1, 0)
            arrived(n, held).wait_recv()
            send(n, held, (0, 0, 0, 1)).start()

    @pl.loop(1, 4)
    def _(zm):
        along(zm)

    @pl.loop(0, 4)
    def _(zm):
        second(zm)

    @pl.loop(0, 8)
    def _(k):
        third(k)

    @pl.loop(0, 16)
    def _(k):
        for n in pieces:
            arrived(n, (k // 4, (k // 2) % 2, k % 2, 1)).wait_recv()

    for copy in own:
        copy.wait()

    @pl.loop(1, 32)
    def _(k):
        for n in pieces:
            arrived(n, (k // 8, (k // 4) % 2, (k // 2) % 2, k % 2)).wait_send()


def gather_all(shards, devices_all):
    return pl.pallas_call(
        gather_kernel,
        out_shape=[
            jax.ShapeDtypeStruct((devices_all,) + piece.shape, piece.dtype) for piece in shards
        ],
        in_specs=[pl.BlockSpec(memory_space=pl.ANY)] * 5,
        out_specs=[pl.BlockSpec(memory_space=pl.ANY)] * 5,
        scratch_shapes=[
            pltpu.SemaphoreType.DMA((len(PIECES), 32)),
            pltpu.SemaphoreType.DMA((len(PIECES), 32)),
            pltpu.SemaphoreType.DMA((5,)),
        ],
        compiler_params=pltpu.CompilerParams(collective_id=0, has_side_effects=True),
    )(*shards)


def scatter_kernel(*refs):
    grads, sums = refs[:5], refs[5:10]
    helds, comes = refs[10:15], refs[15:20]
    send_sem, recv_sem, load_sem = refs[20:]
    device = lax.axis_index("fsdp")
    pieces = range(len(PIECES))
    sibling = (0, 0, 0, 1)

    def load(n, mask):
        piece = PIECES[n]
        slot = code(mask) // 2
        return pltpu.make_async_copy(
            view(grads[piece[0]], moved(device, *mask), piece),
            view(helds[piece[0]], slot, piece),
            load_sem.at[n, slot],
        )

    def push(n, mask, step, source):
        piece = PIECES[n]
        slot = code(mask)
        return pltpu.make_async_remote_copy(
            src_ref=source,
            dst_ref=view(comes[piece[0]], slot, piece),
            send_sem=send_sem.at[n, slot],
            recv_sem=recv_sem.at[n, slot],
            device_id=(moved(device, *step),),
            device_id_type=MESH,
        )

    def across(n, mask):
        piece = PIECES[n]
        other = mask[:3] + (1,)
        return push(n, other, sibling, view(grads[piece[0]], moved(device, *other), piece))

    def onward(n, mask, step):
        piece = PIECES[n]
        return push(n, mask, step, view(helds[piece[0]], code(mask) // 2, piece))

    def total(n, mask, froms, target=None):
        piece = PIECES[n]
        slot = code(mask) // 2
        load(n, mask).wait()
        for other in froms:
            into = view(comes[piece[0]], code(other), piece)
            push(n, other, sibling, into).wait_recv()
        held = view(helds[piece[0]], slot, piece)
        result = held if target is None else view(sums[piece[0]], None, piece)
        terms = [held] + [view(comes[piece[0]], code(other), piece) for other in froms]
        rows, columns = held.shape
        width = min(columns, 768)
        for begin in range(0, columns, width):
            value = terms[0][:, begin : begin + width].astype(jnp.float32)
            for term in terms[1:]:
                value = value + term[:, begin : begin + width].astype(jnp.float32)
            result[:, begin : begin + width] = value.astype(result.dtype)

    def loads(third, k):
        for n in pieces:
            mask = mask_of(PIECES[n][3], k % 4, 1 - k // 4, third, 0)
            load(n, mask).start()

    def sends(third, k):
        for n in pieces:
            mask = mask_of(PIECES[n][3], k % 4, 1 - k // 4, third, 0)
            across(n, mask).start()

    @pl.loop(0, 8)
    def _(k):
        loads(1, k)

    greet(device)

    @pl.loop(0, 8)
    def _(k):
        sends(1, k)

    @pl.loop(0, 8)
    def _(k):
        loads(0, k)
        sends(0, k)

    @pl.loop(0, 8)
    def _(k):
        for n in pieces:
            order = PIECES[n][3]
            mask = mask_of(order, k % 4, 1 - k // 4, 1, 0)
            total(n, mask, [mask[:3] + (1,)])
            onward(n, mask, mask_of(order, 0, 0, 1, 0)).start()

    @pl.loop(0, 4)
    def _(zm):
        for n in pieces:
            order = PIECES[n][3]
            mask = mask_of(order, zm, 1, 0, 0)
            total(n, mask, [mask[:3] + (1,), mask_of(order, zm, 1, 1, 0)])
            onward(n, mask, mask_of(order, 0, 1, 0, 0)).start()

    @pl.loop(1, 4)
    def _(zm):
        for n in pieces:
            order = PIECES[n][3]
            mask = (zm, 0, 0, 0)
            total(
                n,
                mask,
                [(zm, 0, 0, 1), mask_of(order, zm, 0, 1, 0), mask_of(order, zm, 1, 0, 0)],
            )
            onward(n, mask, mask).start()

    for n in pieces:
        order = PIECES[n][3]
        total(
            n,
            (0, 0, 0, 0),
            [(0, 0, 0, 1), mask_of(order, 0, 0, 1, 0), mask_of(order, 0, 1, 0, 0)]
            + [(zm, 0, 0, 0) for zm in (1, 2, 3)],
            True,
        )

    @pl.loop(1, 32)
    def _(k):
        for n in pieces:
            into = view(comes[PIECES[n][0]], k, PIECES[n])
            push(n, (k // 8, (k // 4) % 2, (k // 2) % 2, k % 2), sibling, into).wait_send()


def scatter_all(grads):
    count = grads[0].shape[0]
    return pl.pallas_call(
        scatter_kernel,
        out_shape=[jax.ShapeDtypeStruct(piece.shape[1:], jnp.float32) for piece in grads],
        in_specs=[pl.BlockSpec(memory_space=pl.ANY)] * 5,
        out_specs=[pl.BlockSpec(memory_space=pltpu.VMEM)] * 5,
        scratch_shapes=[
            pltpu.VMEM((count // 2,) + piece.shape[1:], piece.dtype) for piece in grads
        ]
        + [pltpu.VMEM(piece.shape, piece.dtype) for piece in grads]
        + [
            pltpu.SemaphoreType.DMA((len(PIECES), 32)),
            pltpu.SemaphoreType.DMA((len(PIECES), 32)),
            pltpu.SemaphoreType.DMA((len(PIECES), 16)),
        ],
        compiler_params=pltpu.CompilerParams(
            collective_id=1, has_side_effects=True, vmem_limit_bytes=48 * 1024 * 1024
        ),
    )(*grads)


def pack_small(vectors, rows):
    table = jnp.concatenate([v.reshape(-1, rows) for v in vectors], axis=0)
    return jnp.pad(table, ((0, SMALL_ROWS - table.shape[0]), (0, LANES - rows)))


def gather_params(shards, devices_all):
    vectors = tuple(shards[k] for k in (0, 1, 3, 4, 6, 7, 8, 12, 10))
    matrices = tuple(shards[k] for k in (2, 5, 9, 11))
    rows = vectors[0].shape[0]
    if kernels_fit(devices_all, rows):
        small = pack_small(vectors, rows)
        *full, table = gather_all(matrices + (small,), devices_all)
        full = [piece.reshape((-1,) + piece.shape[2:]) for piece in full]
        ratio = vectors[-1].shape[0] // rows
        table = table[:, : 8 + ratio, :rows].transpose(1, 0, 2)
        small_full = [table[k].reshape(-1) for k in range(8)]
        small_full.append(table[8:].transpose(1, 0, 2).reshape(-1))
    else:
        full = [lax.all_gather(piece, "fsdp", axis=0, tiled=True) for piece in matrices]
        table = lax.all_gather(jnp.concatenate(vectors)[None], "fsdp", axis=0, tiled=True)
        small_full = []
        begin = 0
        for piece in vectors:
            small_full.append(table[:, begin : begin + piece.shape[0]].reshape(-1))
            begin += piece.shape[0]
    return full, small_full


def scatter_grads(matrices, vectors, devices_all):
    rows = vectors[0].shape[0] // devices_all
    if kernels_fit(devices_all, rows):
        table = [v.reshape(devices_all, -1, rows) for v in vectors]
        table = jnp.concatenate(table, axis=1)
        table = jnp.pad(table, ((0, 0), (0, SMALL_ROWS - table.shape[1]), (0, LANES - rows)))
        blocks = [g.astype(jnp.bfloat16).reshape(devices_all, -1, g.shape[1]) for g in matrices]
        *full, table = scatter_all(blocks + [table])
        small = [table[k, :rows] for k in range(8)]
        ratio = vectors[-1].shape[0] // vectors[0].shape[0]
        small.append(table[8 : 8 + ratio, :rows].reshape(-1))
        return full, small

    def summed(piece):
        return lax.psum_scatter(piece, "fsdp", scatter_dimension=0, tiled=True)

    return [summed(piece) for piece in matrices], [summed(piece) for piece in vectors]


def kernels_fit(devices_all, rows):
    return devices_all == 32 and rows % 8 == 0 and rows <= LANES


def body(
    tokens,
    cotangent,
    lengths,
    owner,
    offsets,
    ln1_gain,
    ln1_bias,
    w_qkv,
    b_query,
    b_value,
    w_proj,
    b_proj,
    ln2_gain,
    ln2_bias,
    w_fc,
    b_fc,
    w_out,
    b_out,
):
    slot_count, width = tokens.shape
    devices_all = lax.axis_size("fsdp")
    shards = (
        ln1_gain,
        ln1_bias,
        w_qkv,
        b_query,
        b_value,
        w_proj,
        b_proj,
        ln2_gain,
        ln2_bias,
        w_fc,
        b_fc,
        w_out,
        b_out,
    )
    (w_joined, w_project, w_hidden, w_final), (
        gain_one,
        shift_one,
        bias_query,
        bias_value,
        bias_project,
        gain_two,
        shift_two,
        bias_final,
        bias_hidden,
    ) = gather_params(shards, devices_all)
    device = lax.axis_index("fsdp")
    slots = jnp.arange(slot_count, dtype=jnp.int32)
    inside = (
        (owner[:, None] == device)
        & (offsets[:, None] <= slots[None, :])
        & (slots[None, :] < (offsets + lengths)[:, None])
    )
    numbers = jnp.arange(lengths.shape[0], dtype=jnp.int32)[:, None] + 1
    labels = jnp.sum(jnp.where(inside, numbers, 0), axis=0) - 1
    allowed = (labels[:, None] == labels[None, :]) & (slots[None, :] <= slots[:, None])
    valid = (labels >= 0).astype(jnp.float32)
    inputs = tokens.astype(jnp.float32)
    first_out, normal_one, inv_one = norm_forward(
        inputs, gain_one.astype(jnp.float32), shift_one.astype(jnp.float32)
    )
    normed = first_out.astype(jnp.bfloat16)
    joined = jnp.dot(normed, w_joined, preferred_element_type=jnp.float32)
    query = (
        (joined[:, :width] + bias_query.astype(jnp.float32))
        .astype(jnp.bfloat16)
        .reshape(slot_count, H, HD)
    )
    keys = joined[:, width : 2 * width].astype(jnp.bfloat16).reshape(slot_count, H, HD)
    values = (
        (joined[:, 2 * width :] + bias_value.astype(jnp.float32))
        .astype(jnp.bfloat16)
        .reshape(slot_count, H, HD)
    )
    scores = jnp.einsum("qhd,khd->hqk", query, keys, preferred_element_type=jnp.float32) * 0.125
    masked = jnp.where(allowed[None], scores, -1e30)
    row_top = jnp.max(masked, axis=-1, keepdims=True)
    expo = jnp.exp(masked - row_top)
    row_total = jnp.sum(expo, axis=-1, keepdims=True)
    probs = expo / row_total
    log_total = row_top + jnp.log(row_total)
    mixed = (
        jnp.einsum(
            "hqk,khd->qhd", probs.astype(jnp.bfloat16), values, preferred_element_type=jnp.float32
        )
        .reshape(slot_count, width)
        .astype(jnp.bfloat16)
    )
    middle = (
        inputs
        + jnp.dot(mixed, w_project, preferred_element_type=jnp.float32)
        + bias_project.astype(jnp.float32)
    )
    second_out, normal_two, inv_two = norm_forward(
        middle, gain_two.astype(jnp.float32), shift_two.astype(jnp.float32)
    )
    second = second_out.astype(jnp.bfloat16)
    hidden = jnp.dot(second, w_hidden, preferred_element_type=jnp.float32) + bias_hidden.astype(
        jnp.float32
    )
    tanh_part = jnp.tanh(gelu_scale * (hidden + 0.044715 * hidden * hidden * hidden))
    active = (0.5 * hidden * (1.0 + tanh_part)).astype(jnp.bfloat16)
    result = (
        middle
        + jnp.dot(active, w_final, preferred_element_type=jnp.float32)
        + bias_final.astype(jnp.float32)
    )
    grad_result = cotangent.astype(jnp.float32) * valid[:, None]
    grad_low = grad_result.astype(jnp.bfloat16)
    grad_bias_final = column_sum(grad_low)
    grad_w_final = outer_sum(active, grad_low)
    grad_active = through(grad_low, w_final)
    slope = 0.5 * (1.0 + tanh_part) + 0.5 * hidden * (1.0 - tanh_part * tanh_part) * gelu_scale * (
        1.0 + 3.0 * 0.044715 * hidden * hidden
    )
    grad_hidden = (grad_active * slope).astype(jnp.bfloat16)
    grad_bias_hidden = column_sum(grad_hidden)
    grad_w_hidden = outer_sum(second, grad_hidden)
    grad_second = through(grad_hidden, w_hidden)
    norm_grad_two, grad_gain_two, grad_shift_two = norm_backward(
        grad_second, normal_two, inv_two, gain_two.astype(jnp.float32)
    )
    grad_middle = grad_result + norm_grad_two
    grad_branch = grad_middle.astype(jnp.bfloat16)
    grad_bias_project = column_sum(grad_branch)
    grad_w_project = outer_sum(mixed, grad_branch)
    grad_mixed = through(grad_branch, w_project).astype(jnp.bfloat16).reshape(slot_count, H, HD)
    again = jnp.einsum("qhd,khd->hqk", query, keys, preferred_element_type=jnp.float32) * 0.125
    probs_again = jnp.exp(jnp.where(allowed[None], again, -1e30) - log_total)
    grad_probs = jnp.einsum("qhd,khd->hqk", grad_mixed, values, preferred_element_type=jnp.float32)
    grad_values = jnp.einsum(
        "hqk,qhd->khd",
        probs_again.astype(jnp.bfloat16),
        grad_mixed,
        preferred_element_type=jnp.float32,
    )
    row_inner = jnp.sum(grad_probs * probs_again, axis=-1, keepdims=True)
    grad_scores = (probs_again * (grad_probs - row_inner)).astype(jnp.bfloat16)
    grad_query = (
        jnp.einsum("hqk,khd->qhd", grad_scores, keys, preferred_element_type=jnp.float32) * 0.125
    )
    grad_keys = (
        jnp.einsum("hqk,qhd->khd", grad_scores, query, preferred_element_type=jnp.float32) * 0.125
    )
    grad_query = grad_query.astype(jnp.bfloat16).reshape(slot_count, width)
    grad_keys = grad_keys.astype(jnp.bfloat16).reshape(slot_count, width)
    grad_values = grad_values.astype(jnp.bfloat16).reshape(slot_count, width)
    grad_bias_query = column_sum(grad_query)
    grad_bias_value = column_sum(grad_values)
    grad_joined = jnp.concatenate([grad_query, grad_keys, grad_values], axis=1)
    grad_w_joined = outer_sum(normed, grad_joined)
    grad_normed = through(grad_joined, w_joined)
    norm_grad_one, grad_gain_one, grad_shift_one = norm_backward(
        grad_normed, normal_one, inv_one, gain_one.astype(jnp.float32)
    )
    grad_inputs = grad_middle + norm_grad_one
    full, small = scatter_grads(
        (grad_w_joined, grad_w_project, grad_w_hidden, grad_w_final),
        (
            grad_gain_one,
            grad_shift_one,
            grad_bias_query,
            grad_bias_value,
            grad_bias_project,
            grad_gain_two,
            grad_shift_two,
            grad_bias_final,
            grad_bias_hidden,
        ),
        devices_all,
    )
    return (
        result.astype(jnp.bfloat16),
        grad_inputs.astype(jnp.bfloat16),
        small[0],
        small[1],
        full[0],
        small[2],
        small[3],
        full[1],
        small[4],
        small[5],
        small[6],
        full[2],
        small[8],
        full[3],
        small[7],
    )


def solution(mesh):
    in_specs = (
        P("fsdp", None),
        P("fsdp", None),
        P(),
        P(),
        P(),
        P("fsdp"),
        P("fsdp"),
        P("fsdp", None),
        P("fsdp"),
        P("fsdp"),
        P("fsdp", None),
        P("fsdp"),
        P("fsdp"),
        P("fsdp"),
        P("fsdp", None),
        P("fsdp"),
        P("fsdp", None),
        P("fsdp"),
    )
    out_specs = (
        P("fsdp", None),
        P("fsdp", None),
        P("fsdp"),
        P("fsdp"),
        P("fsdp", None),
        P("fsdp"),
        P("fsdp"),
        P("fsdp", None),
        P("fsdp"),
        P("fsdp"),
        P("fsdp"),
        P("fsdp", None),
        P("fsdp"),
        P("fsdp", None),
        P("fsdp"),
    )
    return jax.shard_map(body, mesh=mesh, in_specs=in_specs, out_specs=out_specs, check_vma=False)
```

```python
import jax
import jax.numpy as jnp
from jax import lax
from jax.experimental import pallas as pl
from jax.experimental.pallas import tpu as pltpu
from jax.sharding import PartitionSpec as P

H = 12
HD = 64


gelu_scale = 0.7978845608028654


def norm_forward(values, gain, shift):
    center = values - jnp.mean(values, axis=-1, keepdims=True)
    inv_std = lax.rsqrt(jnp.mean(center * center, axis=-1, keepdims=True) + 1e-05)
    normal = center * inv_std
    return (normal * gain + shift, normal, inv_std)


def norm_backward(upstream, normal, inv_std, gain):
    grad_gain = jnp.sum(upstream * normal, axis=0)
    grad_shift = jnp.sum(upstream, axis=0)
    scaled = upstream * gain
    inner = (
        scaled
        - jnp.mean(scaled, axis=-1, keepdims=True)
        - normal * jnp.mean(scaled * normal, axis=-1, keepdims=True)
    )
    return (inner * inv_std, grad_gain, grad_shift)


def outer_sum(left, right):
    return lax.dot_general(
        left, right, (((0,), (0,)), ((), ())), preferred_element_type=jnp.float32
    )


def through(left, weight):
    return lax.dot_general(
        left, weight, (((1,), (1,)), ((), ())), preferred_element_type=jnp.float32
    )


def column_sum(values):
    return jnp.sum(values.astype(jnp.float32), axis=0)


MESH = pl.DeviceIdType.MESH
SMALL_ROWS = 16
LANES = 128

PIECES = (
    (0, 0, None, 0),
    (1, 0, None, 0),
    (3, 0, 2, 0),
    (4, 0, None, 0),
    (2, 0, None, 1),
    (3, 1, 2, 1),
)


def place(device):
    return (device // 8, (device // 4) % 2, (device // 2) % 2, device % 2)


def moved(device, zm, fy, fx, fc):
    z, y, x, c = place(device)
    z_new = ((z // 2 + zm // 2) % 2) * 2 + (z + zm) % 2
    return z_new * 8 + ((y + fy) % 2) * 4 + ((x + fx) % 2) * 2 + (c + fc) % 2


def mask_of(order, zm, second, third, core):
    fy, fx = (second, third) if order == 0 else (third, second)
    return (zm, fy, fx, core)


def code(mask):
    zm, fy, fx, fc = mask
    return zm * 8 + fy * 4 + fx * 2 + fc


def view(ref, lead, piece):
    _, part, parts, _ = piece
    if parts is None:
        return ref.at[lead] if lead is not None else ref
    rows = ref.shape[-2] // parts
    if lead is None:
        return ref.at[pl.ds(part * rows, rows)]
    return ref.at[lead, pl.ds(part * rows, rows)]


def greet(device):
    barrier = pltpu.get_barrier_semaphore()
    peers = [(1, 0, 0, 0), (2, 0, 0, 0), (3, 0, 0, 0), (0, 1, 0, 0), (0, 0, 1, 0), (0, 0, 0, 1)]
    for peer in peers:
        pl.semaphore_signal(
            barrier, inc=1, device_id=(moved(device, *peer),), device_id_type=MESH
        )
    pl.semaphore_wait(barrier, len(peers))


def gather_kernel(*refs):
    shards, wholes = refs[:5], refs[5:10]
    send_sem, recv_sem, own_sem = refs[10:]
    device = lax.axis_index("fsdp")
    greet(device)

    def send(number, held, step):
        piece = PIECES[number]
        whole = wholes[piece[0]]
        origin = moved(device, *held)
        slot = code(held) + code(step)
        mine = isinstance(held[0], int) and held == (0, 0, 0, 0)
        source = view(shards[piece[0]], None, piece) if mine else view(whole, origin, piece)
        return pltpu.make_async_remote_copy(
            src_ref=source,
            dst_ref=view(whole, origin, piece),
            send_sem=send_sem.at[number, slot],
            recv_sem=recv_sem.at[number, slot],
            device_id=(moved(device, *step),),
            device_id_type=MESH,
        )

    def arrived(number, mask):
        piece = PIECES[number]
        target = view(wholes[piece[0]], moved(device, *mask), piece)
        return pltpu.make_async_remote_copy(
            src_ref=target,
            dst_ref=target,
            send_sem=send_sem.at[number, code(mask)],
            recv_sem=recv_sem.at[number, code(mask)],
            device_id=(moved(device, 0, 0, 0, 1),),
            device_id_type=MESH,
        )

    own = [
        pltpu.make_async_copy(shards[k], wholes[k].at[device], own_sem.at[k]) for k in range(5)
    ]
    home = (0, 0, 0, 0)
    pieces = range(len(PIECES))
    for n in pieces:
        order = PIECES[n][3]
        send(n, home, (1, 0, 0, 0)).start()
        send(n, home, mask_of(order, 0, 1, 0, 0)).start()
        send(n, home, mask_of(order, 0, 0, 1, 0)).start()
    for step in (2, 3):
        for n in pieces:
            send(n, home, (step, 0, 0, 0)).start()
    for n in pieces:
        send(n, home, (0, 0, 0, 1)).start()
    for copy in own:
        copy.start()

    def second(zm):
        for n in pieces:
            order = PIECES[n][3]
            held = mask_of(order, zm, 1, 0, 0)
            arrived(n, held).wait_recv()
            send(n, held, mask_of(order, 0, 0, 1, 0)).start()
            send(n, held, (0, 0, 0, 1)).start()

    def along(zm):
        for n in pieces:
            order = PIECES[n][3]
            held = (zm, 0, 0, 0)
            arrived(n, held).wait_recv()
            send(n, held, mask_of(order, 0, 1, 0, 0)).start()
            send(n, held, mask_of(order, 0, 0, 1, 0)).start()
            send(n, held, (0, 0, 0, 1)).start()

    def third(zm):
        for bit in (0, 1):
            for n in pieces:
                held = mask_of(PIECES[n][3], zm, bit, 1, 0)
                arrived(n, held).wait_recv()
                send(n, held, (0, 0, 0, 1)).start()

    @pl.loop(1, 4)
    def _(zm):
        along(zm)
        second(zm - 1)

        @pl.when(zm >= 2)
        def _():
            third(zm - 2)

    second(3)

    @pl.loop(2, 4)
    def _(zm):
        third(zm)

    @pl.loop(0, 16)
    def _(k):
        for n in pieces:
            arrived(n, (k // 4, (k // 2) % 2, k % 2, 1)).wait_recv()

    for copy in own:
        copy.wait()

    @pl.loop(1, 32)
    def _(k):
        for n in pieces:
            arrived(n, (k // 8, (k // 4) % 2, (k // 2) % 2, k % 2)).wait_send()


def gather_all(shards, devices_all):
    return pl.pallas_call(
        gather_kernel,
        out_shape=[
            jax.ShapeDtypeStruct((devices_all,) + piece.shape, piece.dtype) for piece in shards
        ],
        in_specs=[pl.BlockSpec(memory_space=pl.ANY)] * 5,
        out_specs=[pl.BlockSpec(memory_space=pl.ANY)] * 5,
        scratch_shapes=[
            pltpu.SemaphoreType.DMA((len(PIECES), 32)),
            pltpu.SemaphoreType.DMA((len(PIECES), 32)),
            pltpu.SemaphoreType.DMA((5,)),
        ],
        compiler_params=pltpu.CompilerParams(collective_id=0, has_side_effects=True),
    )(*shards)


def scatter_kernel(*refs):
    grads, sums = refs[:5], refs[5:10]
    helds, comes = refs[10:15], refs[15:20]
    send_sem, recv_sem, load_sem = refs[20:]
    device = lax.axis_index("fsdp")
    pieces = range(len(PIECES))
    sibling = (0, 0, 0, 1)

    def load(n, mask):
        piece = PIECES[n]
        slot = code(mask) // 2
        return pltpu.make_async_copy(
            view(grads[piece[0]], moved(device, *mask), piece),
            view(helds[piece[0]], slot, piece),
            load_sem.at[n, slot],
        )

    def push(n, mask, step, source):
        piece = PIECES[n]
        slot = code(mask)
        return pltpu.make_async_remote_copy(
            src_ref=source,
            dst_ref=view(comes[piece[0]], slot, piece),
            send_sem=send_sem.at[n, slot],
            recv_sem=recv_sem.at[n, slot],
            device_id=(moved(device, *step),),
            device_id_type=MESH,
        )

    def across(n, mask):
        piece = PIECES[n]
        other = mask[:3] + (1,)
        return push(n, other, sibling, view(grads[piece[0]], moved(device, *other), piece))

    def onward(n, mask, step):
        piece = PIECES[n]
        return push(n, mask, step, view(helds[piece[0]], code(mask) // 2, piece))

    def total(n, mask, froms, target=None):
        piece = PIECES[n]
        slot = code(mask) // 2
        load(n, mask).wait()
        for other in froms:
            into = view(comes[piece[0]], code(other), piece)
            push(n, other, sibling, into).wait_recv()
        held = view(helds[piece[0]], slot, piece)
        result = held if target is None else view(sums[piece[0]], None, piece)
        terms = [held] + [view(comes[piece[0]], code(other), piece) for other in froms]
        rows, columns = held.shape
        width = min(columns, 768)
        for begin in range(0, columns, width):
            value = terms[0][:, begin : begin + width].astype(jnp.float32)
            for term in terms[1:]:
                value = value + term[:, begin : begin + width].astype(jnp.float32)
            result[:, begin : begin + width] = value.astype(result.dtype)

    def begin(zm, action):
        for third, second in ((1, 1), (1, 0), (0, 1), (0, 0)):
            for n in pieces:
                action(n, mask_of(PIECES[n][3], zm, second, third, 0)).start()

    @pl.loop(0, 4)
    def _(k):
        begin(3 - k, load)

    greet(device)

    @pl.loop(0, 4)
    def _(k):
        begin(3 - k, across)

    def first_sums(zm):
        for second in (1, 0):
            for n in pieces:
                order = PIECES[n][3]
                mask = mask_of(order, zm, second, 1, 0)
                total(n, mask, [mask[:3] + (1,)])
                onward(n, mask, mask_of(order, 0, 0, 1, 0)).start()

    def second_sums(zm):
        for n in pieces:
            order = PIECES[n][3]
            mask = mask_of(order, zm, 1, 0, 0)
            total(n, mask, [mask[:3] + (1,), mask_of(order, zm, 1, 1, 0)])
            onward(n, mask, mask_of(order, 0, 1, 0, 0)).start()

    def third_sums(zm):
        for n in pieces:
            order = PIECES[n][3]
            mask = (zm, 0, 0, 0)
            total(
                n,
                mask,
                [(zm, 0, 0, 1), mask_of(order, zm, 0, 1, 0), mask_of(order, zm, 1, 0, 0)],
            )
            onward(n, mask, mask).start()

    @pl.loop(0, 6)
    def _(k):
        @pl.when(k < 4)
        def _():
            first_sums(3 - k)

        @pl.when((k >= 1) & (k < 5))
        def _():
            second_sums(4 - k)

        @pl.when((k >= 2) & (k < 5))
        def _():
            third_sums(5 - k)

    for n in pieces:
        order = PIECES[n][3]
        total(
            n,
            (0, 0, 0, 0),
            [(0, 0, 0, 1), mask_of(order, 0, 0, 1, 0), mask_of(order, 0, 1, 0, 0)]
            + [(zm, 0, 0, 0) for zm in (1, 2, 3)],
            True,
        )

    @pl.loop(1, 32)
    def _(k):
        for n in pieces:
            into = view(comes[PIECES[n][0]], k, PIECES[n])
            push(n, (k // 8, (k // 4) % 2, (k // 2) % 2, k % 2), sibling, into).wait_send()


def scatter_all(grads):
    count = grads[0].shape[0]
    return pl.pallas_call(
        scatter_kernel,
        out_shape=[jax.ShapeDtypeStruct(piece.shape[1:], jnp.float32) for piece in grads],
        in_specs=[pl.BlockSpec(memory_space=pl.ANY)] * 5,
        out_specs=[pl.BlockSpec(memory_space=pltpu.VMEM)] * 5,
        scratch_shapes=[
            pltpu.VMEM((count // 2,) + piece.shape[1:], piece.dtype) for piece in grads
        ]
        + [pltpu.VMEM(piece.shape, piece.dtype) for piece in grads]
        + [
            pltpu.SemaphoreType.DMA((len(PIECES), 32)),
            pltpu.SemaphoreType.DMA((len(PIECES), 32)),
            pltpu.SemaphoreType.DMA((len(PIECES), 16)),
        ],
        compiler_params=pltpu.CompilerParams(
            collective_id=1, has_side_effects=True, vmem_limit_bytes=48 * 1024 * 1024
        ),
    )(*grads)


def pack_small(vectors, rows):
    table = jnp.concatenate([v.reshape(-1, rows) for v in vectors], axis=0)
    return jnp.pad(table, ((0, SMALL_ROWS - table.shape[0]), (0, LANES - rows)))


def gather_params(shards, devices_all):
    vectors = tuple(shards[k] for k in (0, 1, 3, 4, 6, 7, 8, 12, 10))
    matrices = tuple(shards[k] for k in (2, 5, 9, 11))
    rows = vectors[0].shape[0]
    if kernels_fit(devices_all, rows):
        small = pack_small(vectors, rows)
        *full, table = gather_all(matrices + (small,), devices_all)
        full = [piece.reshape((-1,) + piece.shape[2:]) for piece in full]
        ratio = vectors[-1].shape[0] // rows
        table = table[:, : 8 + ratio, :rows].transpose(1, 0, 2)
        small_full = [table[k].reshape(-1) for k in range(8)]
        small_full.append(table[8:].transpose(1, 0, 2).reshape(-1))
    else:
        full = [lax.all_gather(piece, "fsdp", axis=0, tiled=True) for piece in matrices]
        table = lax.all_gather(jnp.concatenate(vectors)[None], "fsdp", axis=0, tiled=True)
        small_full = []
        begin = 0
        for piece in vectors:
            small_full.append(table[:, begin : begin + piece.shape[0]].reshape(-1))
            begin += piece.shape[0]
    return full, small_full


def scatter_grads(matrices, vectors, devices_all):
    rows = vectors[0].shape[0] // devices_all
    if kernels_fit(devices_all, rows):
        table = [v.reshape(devices_all, -1, rows) for v in vectors]
        table = jnp.concatenate(table, axis=1)
        table = jnp.pad(table, ((0, 0), (0, SMALL_ROWS - table.shape[1]), (0, LANES - rows)))
        blocks = [g.astype(jnp.bfloat16).reshape(devices_all, -1, g.shape[1]) for g in matrices]
        *full, table = scatter_all(blocks + [table])
        small = [table[k, :rows] for k in range(8)]
        ratio = vectors[-1].shape[0] // vectors[0].shape[0]
        small.append(table[8 : 8 + ratio, :rows].reshape(-1))
        return full, small

    def summed(piece):
        return lax.psum_scatter(piece, "fsdp", scatter_dimension=0, tiled=True)

    return [summed(piece) for piece in matrices], [summed(piece) for piece in vectors]


def kernels_fit(devices_all, rows):
    return devices_all == 32 and rows % 8 == 0 and rows <= LANES


def body(
    tokens,
    cotangent,
    lengths,
    owner,
    offsets,
    ln1_gain,
    ln1_bias,
    w_qkv,
    b_query,
    b_value,
    w_proj,
    b_proj,
    ln2_gain,
    ln2_bias,
    w_fc,
    b_fc,
    w_out,
    b_out,
):
    slot_count, width = tokens.shape
    devices_all = lax.axis_size("fsdp")
    shards = (
        ln1_gain,
        ln1_bias,
        w_qkv,
        b_query,
        b_value,
        w_proj,
        b_proj,
        ln2_gain,
        ln2_bias,
        w_fc,
        b_fc,
        w_out,
        b_out,
    )
    (w_joined, w_project, w_hidden, w_final), (
        gain_one,
        shift_one,
        bias_query,
        bias_value,
        bias_project,
        gain_two,
        shift_two,
        bias_final,
        bias_hidden,
    ) = gather_params(shards, devices_all)
    device = lax.axis_index("fsdp")
    slots = jnp.arange(slot_count, dtype=jnp.int32)
    inside = (
        (owner[:, None] == device)
        & (offsets[:, None] <= slots[None, :])
        & (slots[None, :] < (offsets + lengths)[:, None])
    )
    numbers = jnp.arange(lengths.shape[0], dtype=jnp.int32)[:, None] + 1
    labels = jnp.sum(jnp.where(inside, numbers, 0), axis=0) - 1
    allowed = (labels[:, None] == labels[None, :]) & (slots[None, :] <= slots[:, None])
    valid = (labels >= 0).astype(jnp.float32)
    inputs = tokens.astype(jnp.float32)
    first_out, normal_one, inv_one = norm_forward(
        inputs, gain_one.astype(jnp.float32), shift_one.astype(jnp.float32)
    )
    normed = first_out.astype(jnp.bfloat16)
    joined = jnp.dot(normed, w_joined, preferred_element_type=jnp.float32)
    query = (
        (joined[:, :width] + bias_query.astype(jnp.float32))
        .astype(jnp.bfloat16)
        .reshape(slot_count, H, HD)
    )
    keys = joined[:, width : 2 * width].astype(jnp.bfloat16).reshape(slot_count, H, HD)
    values = (
        (joined[:, 2 * width :] + bias_value.astype(jnp.float32))
        .astype(jnp.bfloat16)
        .reshape(slot_count, H, HD)
    )
    scores = jnp.einsum("qhd,khd->hqk", query, keys, preferred_element_type=jnp.float32) * 0.125
    masked = jnp.where(allowed[None], scores, -1e30)
    row_top = jnp.max(masked, axis=-1, keepdims=True)
    expo = jnp.exp(masked - row_top)
    row_total = jnp.sum(expo, axis=-1, keepdims=True)
    probs = expo / row_total
    log_total = row_top + jnp.log(row_total)
    mixed = (
        jnp.einsum(
            "hqk,khd->qhd", probs.astype(jnp.bfloat16), values, preferred_element_type=jnp.float32
        )
        .reshape(slot_count, width)
        .astype(jnp.bfloat16)
    )
    middle = (
        inputs
        + jnp.dot(mixed, w_project, preferred_element_type=jnp.float32)
        + bias_project.astype(jnp.float32)
    )
    second_out, normal_two, inv_two = norm_forward(
        middle, gain_two.astype(jnp.float32), shift_two.astype(jnp.float32)
    )
    second = second_out.astype(jnp.bfloat16)
    hidden = jnp.dot(second, w_hidden, preferred_element_type=jnp.float32) + bias_hidden.astype(
        jnp.float32
    )
    tanh_part = jnp.tanh(gelu_scale * (hidden + 0.044715 * hidden * hidden * hidden))
    active = (0.5 * hidden * (1.0 + tanh_part)).astype(jnp.bfloat16)
    result = (
        middle
        + jnp.dot(active, w_final, preferred_element_type=jnp.float32)
        + bias_final.astype(jnp.float32)
    )
    grad_result = cotangent.astype(jnp.float32) * valid[:, None]
    grad_low = grad_result.astype(jnp.bfloat16)
    grad_bias_final = column_sum(grad_low)
    grad_w_final = outer_sum(active, grad_low)
    grad_active = through(grad_low, w_final)
    slope = 0.5 * (1.0 + tanh_part) + 0.5 * hidden * (1.0 - tanh_part * tanh_part) * gelu_scale * (
        1.0 + 3.0 * 0.044715 * hidden * hidden
    )
    grad_hidden = (grad_active * slope).astype(jnp.bfloat16)
    grad_bias_hidden = column_sum(grad_hidden)
    grad_w_hidden = outer_sum(second, grad_hidden)
    grad_second = through(grad_hidden, w_hidden)
    norm_grad_two, grad_gain_two, grad_shift_two = norm_backward(
        grad_second, normal_two, inv_two, gain_two.astype(jnp.float32)
    )
    grad_middle = grad_result + norm_grad_two
    grad_branch = grad_middle.astype(jnp.bfloat16)
    grad_bias_project = column_sum(grad_branch)
    grad_w_project = outer_sum(mixed, grad_branch)
    grad_mixed = through(grad_branch, w_project).astype(jnp.bfloat16).reshape(slot_count, H, HD)
    again = jnp.einsum("qhd,khd->hqk", query, keys, preferred_element_type=jnp.float32) * 0.125
    probs_again = jnp.exp(jnp.where(allowed[None], again, -1e30) - log_total)
    grad_probs = jnp.einsum("qhd,khd->hqk", grad_mixed, values, preferred_element_type=jnp.float32)
    grad_values = jnp.einsum(
        "hqk,qhd->khd",
        probs_again.astype(jnp.bfloat16),
        grad_mixed,
        preferred_element_type=jnp.float32,
    )
    row_inner = jnp.sum(grad_probs * probs_again, axis=-1, keepdims=True)
    grad_scores = (probs_again * (grad_probs - row_inner)).astype(jnp.bfloat16)
    grad_query = (
        jnp.einsum("hqk,khd->qhd", grad_scores, keys, preferred_element_type=jnp.float32) * 0.125
    )
    grad_keys = (
        jnp.einsum("hqk,qhd->khd", grad_scores, query, preferred_element_type=jnp.float32) * 0.125
    )
    grad_query = grad_query.astype(jnp.bfloat16).reshape(slot_count, width)
    grad_keys = grad_keys.astype(jnp.bfloat16).reshape(slot_count, width)
    grad_values = grad_values.astype(jnp.bfloat16).reshape(slot_count, width)
    grad_bias_query = column_sum(grad_query)
    grad_bias_value = column_sum(grad_values)
    grad_joined = jnp.concatenate([grad_query, grad_keys, grad_values], axis=1)
    grad_w_joined = outer_sum(normed, grad_joined)
    grad_normed = through(grad_joined, w_joined)
    norm_grad_one, grad_gain_one, grad_shift_one = norm_backward(
        grad_normed, normal_one, inv_one, gain_one.astype(jnp.float32)
    )
    grad_inputs = grad_middle + norm_grad_one
    full, small = scatter_grads(
        (grad_w_joined, grad_w_project, grad_w_hidden, grad_w_final),
        (
            grad_gain_one,
            grad_shift_one,
            grad_bias_query,
            grad_bias_value,
            grad_bias_project,
            grad_gain_two,
            grad_shift_two,
            grad_bias_final,
            grad_bias_hidden,
        ),
        devices_all,
    )
    return (
        result.astype(jnp.bfloat16),
        grad_inputs.astype(jnp.bfloat16),
        small[0],
        small[1],
        full[0],
        small[2],
        small[3],
        full[1],
        small[4],
        small[5],
        small[6],
        full[2],
        small[8],
        full[3],
        small[7],
    )


def solution(mesh):
    in_specs = (
        P("fsdp", None),
        P("fsdp", None),
        P(),
        P(),
        P(),
        P("fsdp"),
        P("fsdp"),
        P("fsdp", None),
        P("fsdp"),
        P("fsdp"),
        P("fsdp", None),
        P("fsdp"),
        P("fsdp"),
        P("fsdp"),
        P("fsdp", None),
        P("fsdp"),
        P("fsdp", None),
        P("fsdp"),
    )
    out_specs = (
        P("fsdp", None),
        P("fsdp", None),
        P("fsdp"),
        P("fsdp"),
        P("fsdp", None),
        P("fsdp"),
        P("fsdp"),
        P("fsdp", None),
        P("fsdp"),
        P("fsdp"),
        P("fsdp"),
        P("fsdp", None),
        P("fsdp"),
        P("fsdp", None),
        P("fsdp"),
    )
    return jax.shard_map(body, mesh=mesh, in_specs=in_specs, out_specs=out_specs, check_vma=False)
```

```python
import jax
import jax.numpy as jnp
from jax import lax
from jax.experimental import pallas as pl
from jax.experimental.pallas import tpu as pltpu
from jax.sharding import PartitionSpec as P

H = 12
HD = 64


gelu_scale = 0.7978845608028654


def norm_forward(values, gain, shift):
    center = values - jnp.mean(values, axis=-1, keepdims=True)
    inv_std = lax.rsqrt(jnp.mean(center * center, axis=-1, keepdims=True) + 1e-05)
    normal = center * inv_std
    return (normal * gain + shift, normal, inv_std)


def norm_backward(upstream, normal, inv_std, gain):
    grad_gain = jnp.sum(upstream * normal, axis=0)
    grad_shift = jnp.sum(upstream, axis=0)
    scaled = upstream * gain
    inner = (
        scaled
        - jnp.mean(scaled, axis=-1, keepdims=True)
        - normal * jnp.mean(scaled * normal, axis=-1, keepdims=True)
    )
    return (inner * inv_std, grad_gain, grad_shift)


def outer_sum(left, right):
    return lax.dot_general(
        left, right, (((0,), (0,)), ((), ())), preferred_element_type=jnp.float32
    )


def through(left, weight):
    return lax.dot_general(
        left, weight, (((1,), (1,)), ((), ())), preferred_element_type=jnp.float32
    )


def column_sum(values):
    return jnp.sum(values.astype(jnp.float32), axis=0)


MESH = pl.DeviceIdType.MESH
SMALL_ROWS = 16
LANES = 128

PIECES = (
    (0, 0, None, 0),
    (1, 0, None, 0),
    (3, 0, 2, 0),
    (4, 0, None, 0),
    (2, 0, None, 1),
    (3, 1, 2, 1),
)


def place(device):
    return (device // 8, (device // 4) % 2, (device // 2) % 2, device % 2)


def moved(device, zm, fy, fx, fc):
    z, y, x, c = place(device)
    z_new = ((z // 2 + zm // 2) % 2) * 2 + (z + zm) % 2
    return z_new * 8 + ((y + fy) % 2) * 4 + ((x + fx) % 2) * 2 + (c + fc) % 2


def mask_of(order, zm, second, third, core):
    fy, fx = (second, third) if order == 0 else (third, second)
    return (zm, fy, fx, core)


def code(mask):
    zm, fy, fx, fc = mask
    return zm * 8 + fy * 4 + fx * 2 + fc


def view(ref, lead, piece):
    _, part, parts, _ = piece
    if parts is None:
        return ref.at[lead] if lead is not None else ref
    rows = ref.shape[-2] // parts
    if lead is None:
        return ref.at[pl.ds(part * rows, rows)]
    return ref.at[lead, pl.ds(part * rows, rows)]


def greet(device):
    barrier = pltpu.get_barrier_semaphore()
    peers = [(1, 0, 0, 0), (2, 0, 0, 0), (3, 0, 0, 0), (0, 1, 0, 0), (0, 0, 1, 0), (0, 0, 0, 1)]
    for peer in peers:
        pl.semaphore_signal(
            barrier, inc=1, device_id=(moved(device, *peer),), device_id_type=MESH
        )
    pl.semaphore_wait(barrier, len(peers))


def gather_kernel(*refs):
    shards, wholes = refs[:5], refs[5:10]
    send_sem, recv_sem, own_sem = refs[10:]
    device = lax.axis_index("fsdp")
    greet(device)

    def send(number, held, step):
        piece = PIECES[number]
        whole = wholes[piece[0]]
        origin = moved(device, *held)
        slot = code(held) + code(step)
        mine = isinstance(held[0], int) and held == (0, 0, 0, 0)
        source = view(shards[piece[0]], None, piece) if mine else view(whole, origin, piece)
        return pltpu.make_async_remote_copy(
            src_ref=source,
            dst_ref=view(whole, origin, piece),
            send_sem=send_sem.at[number, slot],
            recv_sem=recv_sem.at[number, slot],
            device_id=(moved(device, *step),),
            device_id_type=MESH,
        )

    def arrived(number, mask):
        piece = PIECES[number]
        target = view(wholes[piece[0]], moved(device, *mask), piece)
        return pltpu.make_async_remote_copy(
            src_ref=target,
            dst_ref=target,
            send_sem=send_sem.at[number, code(mask)],
            recv_sem=recv_sem.at[number, code(mask)],
            device_id=(moved(device, 0, 0, 0, 1),),
            device_id_type=MESH,
        )

    own = [
        pltpu.make_async_copy(shards[k], wholes[k].at[device], own_sem.at[k]) for k in range(5)
    ]
    home = (0, 0, 0, 0)
    pieces = range(len(PIECES))
    for n in pieces:
        order = PIECES[n][3]
        send(n, home, (1, 0, 0, 0)).start()
        send(n, home, mask_of(order, 0, 1, 0, 0)).start()
        send(n, home, mask_of(order, 0, 0, 1, 0)).start()
    for step in (2, 3):
        for n in pieces:
            send(n, home, (step, 0, 0, 0)).start()
    for n in pieces:
        send(n, home, (0, 0, 0, 1)).start()
    for copy in own:
        copy.start()

    def second(zm):
        for n in pieces:
            order = PIECES[n][3]
            held = mask_of(order, zm, 1, 0, 0)
            arrived(n, held).wait_recv()
            send(n, held, mask_of(order, 0, 0, 1, 0)).start()
            send(n, held, (0, 0, 0, 1)).start()

    def along(zm):
        for n in pieces:
            order = PIECES[n][3]
            held = (zm, 0, 0, 0)
            arrived(n, held).wait_recv()
            send(n, held, mask_of(order, 0, 1, 0, 0)).start()
            send(n, held, mask_of(order, 0, 0, 1, 0)).start()
            send(n, held, (0, 0, 0, 1)).start()

    def third(zm):
        for bit in (0, 1):
            for n in pieces:
                held = mask_of(PIECES[n][3], zm, bit, 1, 0)
                arrived(n, held).wait_recv()
                send(n, held, (0, 0, 0, 1)).start()

    @pl.loop(1, 4)
    def _(zm):
        along(zm)
        second(zm - 1)

        @pl.when(zm >= 2)
        def _():
            third(zm - 2)

    second(3)

    @pl.loop(2, 4)
    def _(zm):
        third(zm)

    @pl.loop(0, 16)
    def _(k):
        for n in pieces:
            arrived(n, (k // 4, (k // 2) % 2, k % 2, 1)).wait_recv()

    for copy in own:
        copy.wait()

    @pl.loop(1, 32)
    def _(k):
        for n in pieces:
            arrived(n, (k // 8, (k // 4) % 2, (k // 2) % 2, k % 2)).wait_send()


def gather_all(shards, devices_all):
    return pl.pallas_call(
        gather_kernel,
        out_shape=[
            jax.ShapeDtypeStruct((devices_all,) + piece.shape, piece.dtype) for piece in shards
        ],
        in_specs=[pl.BlockSpec(memory_space=pl.ANY)] * 5,
        out_specs=[pl.BlockSpec(memory_space=pl.ANY)] * 5,
        scratch_shapes=[
            pltpu.SemaphoreType.DMA((len(PIECES), 32)),
            pltpu.SemaphoreType.DMA((len(PIECES), 32)),
            pltpu.SemaphoreType.DMA((5,)),
        ],
        compiler_params=pltpu.CompilerParams(collective_id=0, has_side_effects=True),
    )(*shards)


def scatter_kernel(*refs):
    grads, sums = refs[:5], refs[5:10]
    helds, comes = refs[10:15], refs[15:20]
    send_sem, recv_sem, load_sem = refs[20:]
    device = lax.axis_index("fsdp")
    pieces = range(len(PIECES))
    sibling = (0, 0, 0, 1)

    def load(n, mask):
        piece = PIECES[n]
        slot = code(mask) // 2
        return pltpu.make_async_copy(
            view(grads[piece[0]], moved(device, *mask), piece),
            view(helds[piece[0]], slot, piece),
            load_sem.at[n, slot],
        )

    def push(n, mask, step, source):
        piece = PIECES[n]
        slot = code(mask)
        return pltpu.make_async_remote_copy(
            src_ref=source,
            dst_ref=view(comes[piece[0]], slot, piece),
            send_sem=send_sem.at[n, slot],
            recv_sem=recv_sem.at[n, slot],
            device_id=(moved(device, *step),),
            device_id_type=MESH,
        )

    def across(n, mask):
        piece = PIECES[n]
        other = mask[:3] + (1,)
        return push(n, other, sibling, view(grads[piece[0]], moved(device, *other), piece))

    def onward(n, mask, step):
        piece = PIECES[n]
        return push(n, mask, step, view(helds[piece[0]], code(mask) // 2, piece))

    def total(n, mask, froms, target=None):
        piece = PIECES[n]
        slot = code(mask) // 2
        load(n, mask).wait()
        for other in froms:
            into = view(comes[piece[0]], code(other), piece)
            push(n, other, sibling, into).wait_recv()
        held = view(helds[piece[0]], slot, piece)
        result = held if target is None else view(sums[piece[0]], None, piece)
        terms = [held] + [view(comes[piece[0]], code(other), piece) for other in froms]
        rows, columns = held.shape
        width = min(columns, 768)
        for begin in range(0, columns, width):
            value = terms[0][:, begin : begin + width].astype(jnp.float32)
            for term in terms[1:]:
                value = value + term[:, begin : begin + width].astype(jnp.float32)
            result[:, begin : begin + width] = value.astype(result.dtype)

    def begin(zm, action):
        for third, second in ((1, 1), (1, 0), (0, 1), (0, 0)):
            for n in pieces:
                action(n, mask_of(PIECES[n][3], zm, second, third, 0)).start()

    @pl.loop(0, 4)
    def _(k):
        begin(3 - k, load)

    greet(device)

    @pl.loop(0, 4)
    def _(k):
        begin(3 - k, across)

    def first_sums(zm):
        for second in (1, 0):
            for n in pieces:
                order = PIECES[n][3]
                mask = mask_of(order, zm, second, 1, 0)
                total(n, mask, [mask[:3] + (1,)])
                onward(n, mask, mask_of(order, 0, 0, 1, 0)).start()

    def second_sums(zm):
        for n in pieces:
            order = PIECES[n][3]
            mask = mask_of(order, zm, 1, 0, 0)
            total(n, mask, [mask[:3] + (1,), mask_of(order, zm, 1, 1, 0)])
            onward(n, mask, mask_of(order, 0, 1, 0, 0)).start()

    def third_sums(zm):
        for n in pieces:
            order = PIECES[n][3]
            mask = (zm, 0, 0, 0)
            total(
                n,
                mask,
                [(zm, 0, 0, 1), mask_of(order, zm, 0, 1, 0), mask_of(order, zm, 1, 0, 0)],
            )
            onward(n, mask, mask).start()

    @pl.loop(0, 6)
    def _(k):
        @pl.when(k < 4)
        def _():
            first_sums(3 - k)

        @pl.when((k >= 1) & (k < 5))
        def _():
            second_sums(4 - k)

        @pl.when((k >= 2) & (k < 5))
        def _():
            third_sums(5 - k)

    for n in pieces:
        order = PIECES[n][3]
        total(
            n,
            (0, 0, 0, 0),
            [(0, 0, 0, 1), mask_of(order, 0, 0, 1, 0), mask_of(order, 0, 1, 0, 0)]
            + [(zm, 0, 0, 0) for zm in (1, 2, 3)],
            True,
        )

    @pl.loop(1, 32)
    def _(k):
        for n in pieces:
            into = view(comes[PIECES[n][0]], k, PIECES[n])
            push(n, (k // 8, (k // 4) % 2, (k // 2) % 2, k % 2), sibling, into).wait_send()


def scatter_all(grads):
    count = grads[0].shape[0]
    return pl.pallas_call(
        scatter_kernel,
        out_shape=[jax.ShapeDtypeStruct(piece.shape[1:], jnp.float32) for piece in grads],
        in_specs=[pl.BlockSpec(memory_space=pl.ANY)] * 5,
        out_specs=[pl.BlockSpec(memory_space=pltpu.VMEM)] * 5,
        scratch_shapes=[
            pltpu.VMEM((count // 2,) + piece.shape[1:], piece.dtype) for piece in grads
        ]
        + [pltpu.VMEM(piece.shape, piece.dtype) for piece in grads]
        + [
            pltpu.SemaphoreType.DMA((len(PIECES), 32)),
            pltpu.SemaphoreType.DMA((len(PIECES), 32)),
            pltpu.SemaphoreType.DMA((len(PIECES), 16)),
        ],
        compiler_params=pltpu.CompilerParams(
            collective_id=1, has_side_effects=True, vmem_limit_bytes=48 * 1024 * 1024
        ),
    )(*grads)


def pack_small(vectors, rows):
    table = jnp.concatenate([v.reshape(-1, rows) for v in vectors], axis=0)
    return jnp.pad(table, ((0, SMALL_ROWS - table.shape[0]), (0, LANES - rows)))


def gather_params(shards, devices_all):
    vectors = tuple(shards[k] for k in (0, 1, 3, 4, 6, 7, 8, 12, 10))
    matrices = tuple(shards[k] for k in (2, 5, 9, 11))
    rows = vectors[0].shape[0]
    if kernels_fit(devices_all, rows):
        small = pack_small(vectors, rows)
        *full, table = gather_all(matrices + (small,), devices_all)
        full = [piece.reshape((-1,) + piece.shape[2:]) for piece in full]
        ratio = vectors[-1].shape[0] // rows
        table = table[:, : 8 + ratio, :rows].transpose(1, 0, 2)
        small_full = [table[k].reshape(-1) for k in range(8)]
        small_full.append(table[8:].transpose(1, 0, 2).reshape(-1))
    else:
        full = [lax.all_gather(piece, "fsdp", axis=0, tiled=True) for piece in matrices]
        table = lax.all_gather(jnp.concatenate(vectors)[None], "fsdp", axis=0, tiled=True)
        small_full = []
        begin = 0
        for piece in vectors:
            small_full.append(table[:, begin : begin + piece.shape[0]].reshape(-1))
            begin += piece.shape[0]
    return full, small_full


def scatter_grads(matrices, vectors, devices_all):
    rows = vectors[0].shape[0] // devices_all
    if kernels_fit(devices_all, rows):
        table = [v.reshape(devices_all, -1, rows) for v in vectors]
        table = jnp.concatenate(table, axis=1)
        table = jnp.pad(table, ((0, 0), (0, SMALL_ROWS - table.shape[1]), (0, LANES - rows)))
        blocks = [g.astype(jnp.bfloat16).reshape(devices_all, -1, g.shape[1]) for g in matrices]
        *full, table = scatter_all(blocks + [table])
        small = [table[k, :rows] for k in range(8)]
        ratio = vectors[-1].shape[0] // vectors[0].shape[0]
        small.append(table[8 : 8 + ratio, :rows].reshape(-1))
        return full, small

    def summed(piece):
        return lax.psum_scatter(piece, "fsdp", scatter_dimension=0, tiled=True)

    return [summed(piece) for piece in matrices], [summed(piece) for piece in vectors]


def kernels_fit(devices_all, rows):
    return devices_all == 32 and rows % 8 == 0 and rows <= LANES


def attention_forward_kernel(q_ref, k_ref, v_ref, down_ref, along_ref, out_ref):
    slots, width = q_ref.shape
    rows = lax.broadcasted_iota(jnp.int32, (slots, slots), 0)
    columns = lax.broadcasted_iota(jnp.int32, (slots, slots), 1)
    allowed = (down_ref[...] == along_ref[...]) & (columns <= rows)
    for begin in range(0, width, 2 * HD):
        q2, k2, v2 = (ref[:, begin : begin + 2 * HD] for ref in (q_ref, k_ref, v_ref))
        parts = []
        for half in (0, HD):
            q, k, v = (piece[:, half : half + HD] for piece in (q2, k2, v2))
            masked = jnp.where(allowed, through(q, k) * 0.125, -1e30)
            top = jnp.max(masked, axis=-1, keepdims=True)
            expo = jnp.exp(masked - top)
            probs = expo / jnp.sum(expo, axis=-1, keepdims=True)
            parts.append(
                jnp.dot(probs.astype(jnp.bfloat16), v, preferred_element_type=jnp.float32)
            )
        out_ref[:, begin : begin + 2 * HD] = jnp.concatenate(parts, axis=1).astype(jnp.bfloat16)


def attention_forward(query, keys, values, labels):
    return pl.pallas_call(
        attention_forward_kernel,
        out_shape=jax.ShapeDtypeStruct(query.shape, jnp.bfloat16),
    )(query, keys, values, labels[:, None], labels[None, :])


def attention_backward_kernel(q_ref, k_ref, v_ref, go_ref, down_ref, along_ref, out_ref):
    slots, width = q_ref.shape
    rows = lax.broadcasted_iota(jnp.int32, (slots, slots), 0)
    columns = lax.broadcasted_iota(jnp.int32, (slots, slots), 1)
    allowed = (down_ref[...] == along_ref[...]) & (columns <= rows)

    def plain(left, right):
        return jnp.dot(left, right, preferred_element_type=jnp.float32)

    for begin in range(0, width, 2 * HD):
        q2, k2, v2, go2 = (
            ref[:, begin : begin + 2 * HD] for ref in (q_ref, k_ref, v_ref, go_ref)
        )
        parts = []
        for half in (0, HD):
            q, k, v, go = (piece[:, half : half + HD] for piece in (q2, k2, v2, go2))
            masked = jnp.where(allowed, through(q, k) * 0.125, -1e30)
            top = jnp.max(masked, axis=-1, keepdims=True)
            total = jnp.sum(jnp.exp(masked - top), axis=-1, keepdims=True)
            probs = jnp.exp(masked - (top + jnp.log(total)))
            grad_probs = through(go, v)
            grad_v = outer_sum(probs.astype(jnp.bfloat16), go)
            inner = jnp.sum(grad_probs * probs, axis=-1, keepdims=True)
            grad_scores = (probs * (grad_probs - inner)).astype(jnp.bfloat16)
            parts.append(
                (plain(grad_scores, k) * 0.125, outer_sum(grad_scores, q) * 0.125, grad_v)
            )
        for which in range(3):
            both = jnp.concatenate([parts[0][which], parts[1][which]], axis=1)
            at = which * width + begin
            out_ref[:, at : at + 2 * HD] = both.astype(jnp.bfloat16)


def attention_backward(query, keys, values, grad_mixed, labels):
    slots, width = query.shape
    return pl.pallas_call(
        attention_backward_kernel,
        out_shape=jax.ShapeDtypeStruct((slots, 3 * width), jnp.bfloat16),
    )(query, keys, values, grad_mixed, labels[:, None], labels[None, :])


def body(
    tokens,
    cotangent,
    lengths,
    owner,
    offsets,
    ln1_gain,
    ln1_bias,
    w_qkv,
    b_query,
    b_value,
    w_proj,
    b_proj,
    ln2_gain,
    ln2_bias,
    w_fc,
    b_fc,
    w_out,
    b_out,
):
    slot_count, width = tokens.shape
    devices_all = lax.axis_size("fsdp")
    shards = (
        ln1_gain,
        ln1_bias,
        w_qkv,
        b_query,
        b_value,
        w_proj,
        b_proj,
        ln2_gain,
        ln2_bias,
        w_fc,
        b_fc,
        w_out,
        b_out,
    )
    (w_joined, w_project, w_hidden, w_final), (
        gain_one,
        shift_one,
        bias_query,
        bias_value,
        bias_project,
        gain_two,
        shift_two,
        bias_final,
        bias_hidden,
    ) = gather_params(shards, devices_all)
    device = lax.axis_index("fsdp")
    slots = jnp.arange(slot_count, dtype=jnp.int32)
    inside = (
        (owner[:, None] == device)
        & (offsets[:, None] <= slots[None, :])
        & (slots[None, :] < (offsets + lengths)[:, None])
    )
    numbers = jnp.arange(lengths.shape[0], dtype=jnp.int32)[:, None] + 1
    labels = jnp.sum(jnp.where(inside, numbers, 0), axis=0) - 1
    valid = (labels >= 0).astype(jnp.float32)
    inputs = tokens.astype(jnp.float32)
    first_out, normal_one, inv_one = norm_forward(
        inputs, gain_one.astype(jnp.float32), shift_one.astype(jnp.float32)
    )
    normed = first_out.astype(jnp.bfloat16)
    joined = jnp.dot(normed, w_joined, preferred_element_type=jnp.float32)
    query_flat = (joined[:, :width] + bias_query.astype(jnp.float32)).astype(jnp.bfloat16)
    keys_flat = joined[:, width : 2 * width].astype(jnp.bfloat16)
    values_flat = (joined[:, 2 * width :] + bias_value.astype(jnp.float32)).astype(jnp.bfloat16)
    mixed = attention_forward(query_flat, keys_flat, values_flat, labels)
    middle = (
        inputs
        + jnp.dot(mixed, w_project, preferred_element_type=jnp.float32)
        + bias_project.astype(jnp.float32)
    )
    second_out, normal_two, inv_two = norm_forward(
        middle, gain_two.astype(jnp.float32), shift_two.astype(jnp.float32)
    )
    second = second_out.astype(jnp.bfloat16)
    hidden = jnp.dot(second, w_hidden, preferred_element_type=jnp.float32) + bias_hidden.astype(
        jnp.float32
    )
    tanh_part = jnp.tanh(gelu_scale * (hidden + 0.044715 * hidden * hidden * hidden))
    active = (0.5 * hidden * (1.0 + tanh_part)).astype(jnp.bfloat16)
    result = (
        middle
        + jnp.dot(active, w_final, preferred_element_type=jnp.float32)
        + bias_final.astype(jnp.float32)
    )
    grad_result = cotangent.astype(jnp.float32) * valid[:, None]
    grad_low = grad_result.astype(jnp.bfloat16)
    grad_bias_final = column_sum(grad_low)
    grad_w_final = outer_sum(active, grad_low)
    grad_active = through(grad_low, w_final)
    slope = 0.5 * (1.0 + tanh_part) + 0.5 * hidden * (1.0 - tanh_part * tanh_part) * gelu_scale * (
        1.0 + 3.0 * 0.044715 * hidden * hidden
    )
    grad_hidden = (grad_active * slope).astype(jnp.bfloat16)
    grad_bias_hidden = column_sum(grad_hidden)
    grad_w_hidden = outer_sum(second, grad_hidden)
    grad_second = through(grad_hidden, w_hidden)
    norm_grad_two, grad_gain_two, grad_shift_two = norm_backward(
        grad_second, normal_two, inv_two, gain_two.astype(jnp.float32)
    )
    grad_middle = grad_result + norm_grad_two
    grad_branch = grad_middle.astype(jnp.bfloat16)
    grad_bias_project = column_sum(grad_branch)
    grad_w_project = outer_sum(mixed, grad_branch)
    grad_mixed = through(grad_branch, w_project).astype(jnp.bfloat16)
    grad_joined = attention_backward(query_flat, keys_flat, values_flat, grad_mixed, labels)
    grad_query = grad_joined[:, :width]
    grad_values = grad_joined[:, 2 * width :]
    grad_bias_query = column_sum(grad_query)
    grad_bias_value = column_sum(grad_values)
    grad_w_joined = outer_sum(normed, grad_joined)
    grad_normed = through(grad_joined, w_joined)
    norm_grad_one, grad_gain_one, grad_shift_one = norm_backward(
        grad_normed, normal_one, inv_one, gain_one.astype(jnp.float32)
    )
    grad_inputs = grad_middle + norm_grad_one
    full, small = scatter_grads(
        (grad_w_joined, grad_w_project, grad_w_hidden, grad_w_final),
        (
            grad_gain_one,
            grad_shift_one,
            grad_bias_query,
            grad_bias_value,
            grad_bias_project,
            grad_gain_two,
            grad_shift_two,
            grad_bias_final,
            grad_bias_hidden,
        ),
        devices_all,
    )
    return (
        result.astype(jnp.bfloat16),
        grad_inputs.astype(jnp.bfloat16),
        small[0],
        small[1],
        full[0],
        small[2],
        small[3],
        full[1],
        small[4],
        small[5],
        small[6],
        full[2],
        small[8],
        full[3],
        small[7],
    )


def solution(mesh):
    in_specs = (
        P("fsdp", None),
        P("fsdp", None),
        P(),
        P(),
        P(),
        P("fsdp"),
        P("fsdp"),
        P("fsdp", None),
        P("fsdp"),
        P("fsdp"),
        P("fsdp", None),
        P("fsdp"),
        P("fsdp"),
        P("fsdp"),
        P("fsdp", None),
        P("fsdp"),
        P("fsdp", None),
        P("fsdp"),
    )
    out_specs = (
        P("fsdp", None),
        P("fsdp", None),
        P("fsdp"),
        P("fsdp"),
        P("fsdp", None),
        P("fsdp"),
        P("fsdp"),
        P("fsdp", None),
        P("fsdp"),
        P("fsdp"),
        P("fsdp"),
        P("fsdp", None),
        P("fsdp"),
        P("fsdp", None),
        P("fsdp"),
    )
    return jax.shard_map(body, mesh=mesh, in_specs=in_specs, out_specs=out_specs, check_vma=False)
```
